32 devices in a mesh: dp: 2 (over x), seq: 8 (over z, core), tensor: 2 (over y).
Axes of the slice: x: 2, y: 2, z: 4, core: 2. Of those that a mesh axis runs over, the one named last changes fastest.
Arguments:
- queries: bfloat16 [2, 1024, 3072], P('dp', 'seq', 'tensor'), may hold values from -24 to 24
- keys: bfloat16 [2, 2048, 3072], P('dp', 'seq', 'tensor'), may hold values from -8 to 8
- values: bfloat16 [2, 2048, 3072], P('dp', 'seq', 'tensor'), may hold values from -160 to 160
- grad_out: bfloat16 [2, 1024, 3072], P('dp', 'seq', 'tensor'), may hold values from -60 to 60
- gain: float32 [3072], P('tensor'), may hold values from 0.1 to 1.9
- band_start: int32 [2, 8], P('dp', 'seq'), may hold values from 0 to 14, as said below
- band_end: int32 [2, 8], P('dp', 'seq'), may hold values from 6 to 16
Outputs:
- attended: bfloat16 [2, 1024, 3072], P('dp', 'seq', 'tensor')
- grad_queries: bfloat16 [2, 1024, 3072], P('dp', 'seq', 'tensor')
- grad_keys: bfloat16 [2, 2048, 3072], P('dp', 'seq', 'tensor')
- grad_values: bfloat16 [2, 2048, 3072], P('dp', 'seq', 'tensor')
- grad_gain: float32 [3072], P('tensor')
The draws below stay inside these ranges and needn't reach their ends.
Inputs may be any that keep to these rules, and one draw needn't show every extreme that they name: Along the token blocks of a recording band_start and band_end never fall and band_start < band_end; the band of a token block held by seq index j lies within encoder blocks (j - 2) * (2) to (j + 3) * 2 - 1, and in every draw some bands reach both of these limits.
All inputs are finite; a program needn't handle non-finite values.
Results may differ from the reference program's by a relative error of at most 0.008.
Values may be sent and summed in bfloat16 or wider, within the bound.
A program may use at most 128 MiB of HBM per device.

```python
import math
import jax
import jax.numpy as jnp
from jax import lax

D = 3072
HD = 96
TOK_DEV = 128
F_DEV = 256
TB = 128
EB = 128
REACH = 2
REC = 2
TOKENS = 1024
FRAMES = 2048
NTB = 8
NEB = 16


def draw_queries(key, part):
    key = jax.random.fold_in(key, 101)
    shape = (REC, TOKENS, D)
    base = jax.random.truncated_normal(key, -6.0, 6.0, shape, jnp.float32)
    return base.astype(jnp.bfloat16)


def draw_keys(key, part):
    key = jax.random.fold_in(key, 202)
    shape = (REC, FRAMES, D)
    base = jax.random.truncated_normal(key, -6.0, 6.0, shape, jnp.float32)
    return base.astype(jnp.bfloat16)


def draw_values(key, part):
    key = jax.random.fold_in(key, 303)
    shape = (REC, FRAMES, D)
    key_col = jax.random.fold_in(key, 0)
    key_base = jax.random.fold_in(key, 2)
    column_scale = jnp.exp(jax.random.uniform(key_col, (D,), jnp.float32, 0.0, math.log(10.0)))
    base = jax.random.truncated_normal(key_base, -6.0, 6.0, shape, jnp.float32)
    return (base * column_scale[None, None, :]).astype(jnp.bfloat16)


def draw_grad_out(key, part):
    key = jax.random.fold_in(key, 404)
    shape = (REC, TOKENS, D)
    key_row, key_base = jax.random.split(key, 2)
    row_scale = jnp.exp(jax.random.uniform(key_row, (REC, TOKENS, 1), jnp.float32, 0.0, math.log(10.0)))
    position = jnp.arange(TOKENS, dtype=jnp.float32)[None, :, None] / TOKENS
    base = jax.random.truncated_normal(key_base, -6.0, 6.0, shape, jnp.float32)
    ramp = jnp.exp(position * math.log(3.0))
    return (0.3 * base * row_scale * ramp).astype(jnp.bfloat16)


def band_pair(key):
    shared = jax.random.fold_in(key, 11)
    key_limit, key_low, key_high = jax.random.split(shared, 3)
    per_device = TOK_DEV // TB
    per_encoder = F_DEV // EB
    devices = NTB // per_device
    block = jnp.arange(NTB, dtype=jnp.int32)
    center = block * NEB // NTB
    device = block // per_device
    lowest = jnp.maximum((device - REACH) * per_encoder, 0)
    highest = jnp.minimum((device + REACH + 1) * per_encoder, NEB)
    full = (REACH + 1) * per_encoder
    limit = jax.random.randint(key_limit, (REC, devices), 1, full + 1, jnp.int32)
    limit = jnp.repeat(limit, per_device, axis=1)
    below = jax.random.randint(key_low, (REC, NTB), 0, 1 << 20, jnp.int32) % (limit + 1)
    above = jax.random.randint(key_high, (REC, NTB), 0, 1 << 20, jnp.int32) % (limit + 1)
    forced = block % 7 == 0
    last = block == NTB - 1
    below = jnp.where(forced[None, :], full, below)
    above = jnp.where(forced[None, :] | last[None, :], full, above)
    below = jnp.where(last[None, :], 0, below)
    start = jnp.maximum(lax.cummax(center[None, :] - below, axis=1), lowest[None, :])
    finish = jnp.minimum(lax.cummax(center[None, :] + 1 + above, axis=1), highest[None, :])
    return (start.astype(jnp.int32), finish.astype(jnp.int32))


def draw_band_start(key, part):
    return band_pair(key)[0]


def draw_band_end(key, part):
    return band_pair(key)[1]


def setup_inputs(seed: int = 0) -> dict:
    streams_of = jax.random.split(jax.random.key(seed), 8)
    return {
        "queries": draw_queries(jax.random.fold_in(streams_of[7], 71), 0),
        "keys": draw_keys(jax.random.fold_in(streams_of[7], 71), 0),
        "values": draw_values(jax.random.fold_in(streams_of[7], 71), 0),
        "grad_out": draw_grad_out(jax.random.fold_in(streams_of[7], 71), 0),
        "gain": jnp.clip(1.0 + 0.18 * jax.random.normal(streams_of[4], (D,), jnp.float32), 0.1, 1.9),
        "band_start": draw_band_start(jax.random.fold_in(streams_of[7], 71), 0),
        "band_end": draw_band_end(jax.random.fold_in(streams_of[7], 71), 0),
    }


epsilon = 1e-06

def reference(queries, keys, values, grad_out, gain, band_start, band_end):
    heads = D // HD
    scale = HD ** (-0.5)
    span = (2 * REACH + 1) * F_DEV
    per_device = TOK_DEV // TB
    margin = REACH * F_DEV
    attended_all = []
    grad_query_all = []
    grad_key_all = []
    grad_value_all = []
    gain_total = jnp.zeros((D,), jnp.float32)
    for record in range(REC):
        query_rec = queries[record]
        key_pad = jnp.pad(keys[record], ((margin, margin), (0, 0)))
        value_pad = jnp.pad(values[record], ((margin, margin), (0, 0)))
        grad_rec = grad_out[record]
        starts = band_start[record]
        ends = band_end[record]

        def block_step(carry, block):
            key_acc, value_acc, gain_acc = carry
            device = block // per_device
            first = (device * F_DEV).astype(jnp.int32)
            row_first = (block * TB).astype(jnp.int32)
            query_block = lax.dynamic_slice_in_dim(query_rec, row_first, TB, 0)
            grad_block = lax.dynamic_slice_in_dim(grad_rec, row_first, TB, 0).astype(jnp.float32)
            key_block = lax.dynamic_slice_in_dim(key_pad, first, span, 0)
            value_block = lax.dynamic_slice_in_dim(value_pad, first, span, 0)
            frame_block = ((device - REACH) * F_DEV + jnp.arange(span, dtype=jnp.int32)) // EB
            allowed = (frame_block >= starts[block]) & (frame_block < ends[block])
            query_heads = query_block.astype(jnp.float32).reshape(TB, heads, HD)
            key_heads = key_block.astype(jnp.float32).reshape(span, heads, HD)
            value_heads = value_block.astype(jnp.float32).reshape(span, heads, HD)
            scores = jnp.einsum('qhd,khd->hqk', query_heads, key_heads) * scale
            scores = jnp.where(allowed[None, None, :], scores, -jnp.inf)
            top = lax.optimization_barrier(jnp.max(scores, axis=-1, keepdims=True))
            weights = jnp.exp(scores - top)
            probs = weights / lax.optimization_barrier(jnp.sum(weights, axis=-1, keepdims=True))
            probs_b = lax.optimization_barrier(probs.astype(jnp.bfloat16)).astype(jnp.float32)
            attn = jnp.einsum('hqk,khd->qhd', probs_b, value_heads).reshape(TB, D)
            inv_rms = lax.rsqrt(lax.optimization_barrier(jnp.mean(attn * attn, axis=1)) + epsilon)
            normed = attn * inv_rms[:, None]
            attended = (normed * gain[None, :]).astype(jnp.bfloat16)
            gain_acc = gain_acc + lax.optimization_barrier(jnp.sum(grad_block * normed, axis=0))
            scaled_grad = grad_block * gain[None, :]
            mean_cross = lax.optimization_barrier(jnp.mean(scaled_grad * normed, axis=1))
            grad_attn = (inv_rms[:, None] * (scaled_grad - normed * mean_cross[:, None])).astype(jnp.bfloat16)
            grad_attn_heads = lax.optimization_barrier(grad_attn).astype(jnp.float32).reshape(TB, heads, HD)
            grad_probs = jnp.einsum('qhd,khd->hqk', grad_attn_heads, value_heads)
            inner = lax.optimization_barrier(jnp.sum(probs * grad_probs, axis=-1, keepdims=True))
            grad_scores = lax.optimization_barrier((probs * (grad_probs - inner)).astype(jnp.bfloat16)).astype(jnp.float32)
            grad_query = (scale * jnp.einsum('hqk,khd->qhd', grad_scores, key_heads)).reshape(TB, D).astype(jnp.bfloat16)
            grad_key = (scale * jnp.einsum('hqk,qhd->khd', grad_scores, query_heads)).reshape(span, D)
            grad_value = jnp.einsum('hqk,qhd->khd', probs_b, grad_attn_heads).reshape(span, D)
            key_acc = lax.dynamic_update_slice_in_dim(key_acc, lax.dynamic_slice_in_dim(key_acc, first, span, 0) + grad_key, first, 0)
            value_acc = lax.dynamic_update_slice_in_dim(value_acc, lax.dynamic_slice_in_dim(value_acc, first, span, 0) + grad_value, first, 0)
            return ((key_acc, value_acc, gain_acc), (attended, grad_query))
        start_carry = (jnp.zeros((FRAMES + 2 * margin, D), jnp.float32), jnp.zeros((FRAMES + 2 * margin, D), jnp.float32), jnp.zeros((D,), jnp.float32))
        final, stacked = lax.scan(block_step, start_carry, jnp.arange(NTB, dtype=jnp.int32))
        key_acc, value_acc, gain_acc = final
        gain_total = gain_total + gain_acc
        attended_all.append(stacked[0].reshape(TOKENS, D))
        grad_query_all.append(stacked[1].reshape(TOKENS, D))
        grad_key_all.append(key_acc[margin:margin + FRAMES].astype(jnp.bfloat16))
        grad_value_all.append(value_acc[margin:margin + FRAMES].astype(jnp.bfloat16))
    return (jnp.stack(attended_all), jnp.stack(grad_query_all), jnp.stack(grad_key_all), jnp.stack(grad_value_all), gain_total)
```

```python
import functools

import jax
import jax.numpy as jnp
from jax import lax
from jax.experimental import pallas as pl
from jax.experimental.pallas import tpu as pltpu
from jax.sharding import PartitionSpec as P

D = 3072
HD = 96
EB = 128
GH = 4
GW = GH * HD
OFFS = (-2, 2, -1, 1)
NS = len(OFFS)
OWN = NS
NEG = -1e30
EPS = 1e-06
MESH = pl.DeviceIdType.MESH
F32 = jnp.float32
BF16 = jnp.bfloat16


def dot_nn(a, b):
    return jnp.dot(a, b, preferred_element_type=F32)


def dot_nt(a, b):
    return lax.dot_general(a, b, (((1,), (1,)), ((), ())), preferred_element_type=F32)


def xor_strides(size):
    out = []
    s = 1
    while s < size:
        out.append(s)
        s *= 2
    return out


def xor_partner(index, stride):
    return index + stride - 2 * stride * ((index // stride) % 2)


def body(
    sizes, q_ref, k_ref, v_ref, g_ref, gain_ref, bs_ref, be_ref,
    att_ref, dq_ref, dk_ref, dv_ref, dg_ref,
    qt, qin, band, bandin, kt, vt, kh, vh, e, oown, sown, oout, sout, oin, sin,
    attn, sgt, dot, cown, cout, doin, cin, dqown, dqout, dqin, dkt, dvt, stat, gg, norm,
    q_s, q_r, b_s, b_r, o_s, o_r, s_s, s_r, d_s, d_r, c_s, c_r, x_s, x_r,
    t_s, t_r, gg_s, gg_r,
):
    n_dp, n_seq, n_tensor = sizes
    toks, width = q_ref.shape
    frames = k_ref.shape[0]
    groups = width // GW
    scale = HD ** (-0.5)
    me = lax.axis_index("seq")
    tp = lax.axis_index("tensor")
    dp = lax.axis_index("dp")

    def inside(i):
        return (i >= 0) & (i < n_seq)

    barrier = pltpu.get_barrier_semaphore()
    t_strides = xor_strides(n_tensor)
    gain_stages = [("seq", s) for s in xor_strides(n_seq)] + [("dp", s) for s in xor_strides(n_dp)]
    for i, d in enumerate(OFFS):
        @pl.when(inside(me + d))
        def _(d=d):
            pl.semaphore_signal(barrier, inc=1, device_id={"seq": me + d}, device_id_type=MESH)
    fixed = 0
    for s in t_strides:
        pl.semaphore_signal(barrier, inc=1, device_id={"tensor": xor_partner(tp, s)}, device_id_type=MESH)
        fixed += 1
    for axis, s in gain_stages:
        if axis == "seq" and s > 2:
            pl.semaphore_signal(barrier, inc=1, device_id={"seq": xor_partner(me, s)}, device_id_type=MESH)
            fixed += 1
        if axis == "dp":
            pl.semaphore_signal(barrier, inc=1, device_id={"dp": xor_partner(dp, s)}, device_id_type=MESH)
            fixed += 1

    band[0:4, :] = jnp.full((4, 128), bs_ref[0], jnp.int32)
    band[4:8, :] = jnp.full((4, 128), be_ref[0], jnp.int32)

    def tcols(c):
        return pl.ds(pl.multiple_of(c * 128, 128), 128)

    def q_body(c, _):
        qt[tcols(c), :] = q_ref[:, tcols(c)].T
        return 0
    lax.fori_loop(0, width // 128, q_body, 0)

    peers = jnp.int32(fixed)
    for d in OFFS:
        peers = peers + jnp.where(inside(me + d), 1, 0).astype(jnp.int32)
    pl.semaphore_wait(barrier, peers)

    def rows(g):
        return pl.ds(pl.multiple_of(g * GW, GW), GW)

    def hrows(g, j):
        return pl.ds(pl.multiple_of(g * GW + j * HD, 32), HD)

    def remote(src, dst, ss, rs, to):
        return pltpu.make_async_remote_copy(
            src_ref=src, dst_ref=dst, send_sem=ss, recv_sem=rs,
            device_id={"seq": to}, device_id_type=MESH,
        )

    def q_copy(i, g):
        return remote(qt.at[rows(g)], qin.at[i, rows(g)], q_s.at[i, g], q_r.at[i, g], me + OFFS[i])

    def b_copy(i):
        return remote(band, bandin.at[i], b_s.at[i], b_r.at[i], me + OFFS[i])

    def o_copy(i, g):
        return remote(oout.at[i, rows(g)], oin.at[i, rows(g)], o_s.at[i, g], o_r.at[i, g], me - OFFS[i])

    def s_copy(i, g):
        return remote(sout.at[i, g], sin.at[i, g], s_s.at[i, g], s_r.at[i, g], me - OFFS[i])

    def d_copy(i, g):
        return remote(dot.at[rows(g)], doin.at[i, rows(g)], d_s.at[i, g], d_r.at[i, g], me + OFFS[i])

    def c_copy(i, g):
        return remote(cout.at[i, g], cin.at[i, g], c_s.at[i, g], c_r.at[i, g], me + OFFS[i])

    def x_copy(i, g):
        return remote(dqout.at[i, rows(g)], dqin.at[i, rows(g)], x_s.at[i, g], x_r.at[i, g], me - OFFS[i])

    def to_target(i):
        return pl.when(inside(me + OFFS[i]))

    def to_client(i):
        return pl.when(inside(me - OFFS[i]))

    for i in range(NS):
        @to_target(i)
        def _(i=i):
            b_copy(i).start()

    def q_send(g, _):
        for i in range(NS):
            @to_target(i)
            def _(i=i):
                q_copy(i, g).start()
        return 0
    lax.fori_loop(0, groups, q_send, 0)

    def kv_body(c, _):
        kt[tcols(c), :] = k_ref[:, tcols(c)].T
        vt[tcols(c), :] = v_ref[:, tcols(c)].T
        sgt[tcols(c), :] = (g_ref[:, tcols(c)].astype(F32) * gain_ref[:, tcols(c)]).T
        return 0
    lax.fori_loop(0, width // 128, kv_body, 0)

    def head_body(g, _):
        kg = k_ref[:, rows(g)]
        vg = v_ref[:, rows(g)]
        for j in range(GH):
            kh[g * GH + j] = kg[:, j * HD:(j + 1) * HD]
            vh[g * GH + j] = vg[:, j * HD:(j + 1) * HD]
        return 0
    lax.fori_loop(0, groups, head_body, 0)

    def forward(g, q_at, band_at, slot, o_put, s_put):
        start = band_at[0:1, :]
        end = band_at[4:5, :]
        first = me * (frames // EB)
        bias = []
        for b in range(frames // EB):
            ok = (first + b >= start) & (first + b < end)
            bias.append(jnp.where(ok, 0.0, NEG).astype(F32))
        for j in range(GH):
            h = g * GH + j
            s = dot_nn(kh[h], q_at[hrows(g, j), :]) * scale
            s = jnp.concatenate([s[b * EB:(b + 1) * EB] + bias[b] for b in range(frames // EB)], axis=0)
            top = jnp.max(s, axis=0, keepdims=True)
            w = jnp.exp(s - top)
            e[slot, h] = w
            s_put(g, j, top, jnp.sum(w, axis=0, keepdims=True))
            o_put(g, j, dot_nn(vt[hrows(g, j), :], w.astype(BF16)))

    def own_fwd(g, _):
        def o_put(g, j, o):
            oown[hrows(g, j), :] = o

        def s_put(g, j, top, total):
            sown[g, j:j + 1, :] = top
            sown[g, GH + j:GH + j + 1, :] = total
        forward(g, qt, band, OWN, o_put, s_put)
        return 0
    lax.fori_loop(0, groups, own_fwd, 0)

    for i in range(NS):
        @pl.when(jnp.logical_not(inside(me + OFFS[i])))
        def _(i=i):
            oin[i] = jnp.zeros(oin.shape[1:], BF16)
            sin[i, :, 0:GH, :] = jnp.full((groups, GH, toks), NEG, F32)
            sin[i, :, GH:, :] = jnp.zeros((groups, GH, toks), F32)
            dqin[i] = jnp.zeros(dqin.shape[1:], BF16)

    for i in range(NS):
        @to_client(i)
        def _(i=i):
            b_copy(i).wait_recv()

    def serve_fwd(g, _):
        for i in range(NS):
            @to_client(i)
            def _(i=i):
                q_copy(i, g).wait_recv()

                def o_put(g, j, o):
                    oout[i, hrows(g, j), :] = o.astype(BF16)

                def s_put(g, j, top, total):
                    sout[i, g, j:j + 1, :] = top
                    sout[i, g, GH + j:GH + j + 1, :] = total
                forward(g, qin.at[i], bandin.at[i], i, o_put, s_put)
                s_copy(i, g).start()
                o_copy(i, g).start()
        return 0
    lax.fori_loop(0, groups, serve_fwd, 0)

    def fold(x):
        return jnp.sum(x.reshape(x.shape[0] // 8, 8, x.shape[1]), axis=0)

    def combine(g, carry):
        square, cross = carry
        for i in range(NS):
            @to_target(i)
            def _(i=i):
                s_copy(i, g).wait_recv()
                o_copy(i, g).wait_recv()
        for j in range(GH):
            tops = [sin[i, g, j:j + 1, :] for i in range(NS)] + [sown[g, j:j + 1, :]]
            sums = [sin[i, g, GH + j:GH + j + 1, :] for i in range(NS)] + [sown[g, GH + j:GH + j + 1, :]]
            top = functools.reduce(jnp.maximum, tops)
            ws = [jnp.exp(t - top) for t in tops]
            total = functools.reduce(lambda a, b: a + b, [w * x for w, x in zip(ws, sums)])
            inv = 1.0 / total
            cs = [w * inv for w in ws]
            acc = oown[hrows(g, j), :] * cs[OWN]
            for i in range(NS):
                acc = acc + oin[i, hrows(g, j), :].astype(F32) * cs[i]
                cout[i, g, j:j + 1, :] = cs[i]
            cown[g, j:j + 1, :] = cs[OWN]
            attn[hrows(g, j), :] = acc
            square = square + fold(acc * acc)
            cross = cross + fold(acc * sgt[hrows(g, j), :])
        return square, cross
    zero = jnp.zeros((8, toks), F32)
    square, cross = lax.fori_loop(0, groups, combine, (zero, zero))

    stat[0, 0:8, :] = square
    stat[0, 8:16, :] = cross
    for number, s in enumerate(t_strides):
        copy = pltpu.make_async_remote_copy(
            src_ref=stat.at[2 * number], dst_ref=stat.at[2 * number + 1],
            send_sem=t_s.at[number], recv_sem=t_r.at[number],
            device_id={"tensor": xor_partner(tp, s)}, device_id_type=MESH,
        )
        copy.start()
        copy.wait()
        stat[2 * number + 2] = stat[2 * number] + stat[2 * number + 1]
    last = 2 * len(t_strides)
    square = jnp.sum(stat[last, 0:8, :], axis=0, keepdims=True)
    cross = jnp.sum(stat[last, 8:16, :], axis=0, keepdims=True)
    inv_rms = lax.rsqrt(square / D + EPS)
    mean_cross = inv_rms * cross / D

    def grad_attn(g, _):
        for j in range(GH):
            a = attn[hrows(g, j), :]
            normed = a * inv_rms
            norm[hrows(g, j), :] = normed
            da = (inv_rms * (sgt[hrows(g, j), :] - normed * mean_cross)).astype(BF16)
            dot[hrows(g, j), :] = da
            inner = jnp.sum(da.astype(F32) * a, axis=0, keepdims=True)
            cown[g, GH + j:GH + j + 1, :] = inner
            for i in range(NS):
                cout[i, g, GH + j:GH + j + 1, :] = inner
        for i in range(NS):
            @to_target(i)
            def _(i=i):
                c_copy(i, g).start()
                d_copy(i, g).start()
        return 0
    lax.fori_loop(0, groups, grad_attn, 0)

    def att_body(c, _):
        normed = norm[tcols(c), :].T
        att_ref[:, tcols(c)] = (normed * gain_ref[:, tcols(c)]).astype(BF16)
        gg[0, :, tcols(c)] = fold(normed * g_ref[:, tcols(c)].astype(F32))
        return 0
    lax.fori_loop(0, width // 128, att_body, 0)

    def gain_copy(number):
        axis, s = gain_stages[number]
        index = me if axis == "seq" else dp
        return pltpu.make_async_remote_copy(
            src_ref=gg.at[2 * number], dst_ref=gg.at[2 * number + 1],
            send_sem=gg_s.at[number], recv_sem=gg_r.at[number],
            device_id={axis: xor_partner(index, s)}, device_id_type=MESH,
        )

    def gain_finish(number):
        gain_copy(number).wait()
        gg[2 * number + 2] = gg[2 * number] + gg[2 * number + 1]

    def backward(g, q_at, d_at, c_at, slot, dq_put, first):
        for j in range(GH):
            h = g * GH + j
            q = q_at[hrows(g, j), :]
            da = d_at[hrows(g, j), :]
            p = e[slot, h] * c_at[g, j:j + 1, :]
            pb = p.astype(BF16)
            dp_ = dot_nn(vh[h], da)
            ds = (p * (dp_ - c_at[g, GH + j:GH + j + 1, :])).astype(BF16)
            dk = dot_nt(q, ds)
            dv = dot_nt(da, pb)
            if first:
                dkt[hrows(g, j), :] = dk
                dvt[hrows(g, j), :] = dv
            else:
                dkt[hrows(g, j), :] += dk
                dvt[hrows(g, j), :] += dv
            dq_put(g, j, dot_nn(kt[hrows(g, j), :], ds) * scale)

    def own_put(g, j, x):
        dqown[hrows(g, j), :] = x

    stages = len(gain_stages)
    gain_copy(0).start()
    for g in range(groups):
        backward(g, qt, dot, cown, OWN, own_put, True)
        if g < stages:
            gain_finish(g)
            if g + 1 < stages:
                gain_copy(g + 1).start()

    def serve_bwd(g, _):
        for i in range(NS):
            @to_client(i)
            def _(i=i):
                c_copy(i, g).wait_recv()
                d_copy(i, g).wait_recv()

                def put(g, j, x):
                    dqout[i, hrows(g, j), :] = x.astype(BF16)
                backward(g, qin.at[i], doin.at[i], cin.at[i], i, put, False)
                x_copy(i, g).start()
        return 0
    lax.fori_loop(0, groups, serve_bwd, 0)

    for number in range(groups, stages):
        gain_finish(number)
        if number + 1 < stages:
            gain_copy(number + 1).start()
    dg_ref[...] = jnp.sum(gg[2 * stages], axis=0, keepdims=True)

    def out_kv(c, _):
        dk_ref[:, tcols(c)] = (dkt[tcols(c), :] * scale).astype(BF16).T
        dv_ref[:, tcols(c)] = dvt[tcols(c), :].astype(BF16).T
        return 0
    lax.fori_loop(0, width // 128, out_kv, 0)

    def out_q(g, _):
        for i in range(NS):
            @to_target(i)
            def _(i=i):
                x_copy(i, g).wait_recv()
        for c in range(GW // 128):
            at = tcols(g * (GW // 128) + c)
            acc = dqown[at, :]
            for i in range(NS):
                acc = acc + dqin[i, at, :].astype(F32)
            dq_ref[:, at] = acc.astype(BF16).T
        return 0
    lax.fori_loop(0, groups, out_q, 0)

    def drain(g, _):
        for i in range(NS):
            @to_target(i)
            def _(i=i):
                q_copy(i, g).wait_send()
                c_copy(i, g).wait_send()
                d_copy(i, g).wait_send()

            @to_client(i)
            def _(i=i):
                o_copy(i, g).wait_send()
                s_copy(i, g).wait_send()
                x_copy(i, g).wait_send()
        return 0
    lax.fori_loop(0, groups, drain, 0)
    for i in range(NS):
        @to_target(i)
        def _(i=i):
            b_copy(i).wait_send()


def per_device(sizes, queries, keys, values, grad_out, gain, band_start, band_end):
    toks, width = queries.shape[1:]
    frames = keys.shape[1]
    heads = width // HD
    groups = width // GW
    n_dp, n_seq, n_tensor = sizes
    n_t = len(xor_strides(n_tensor))
    n_g = len(xor_strides(n_seq)) + len(xor_strides(n_dp))
    vm = pltpu.VMEM
    slots = (NS, width, toks)
    rows8 = (groups, 8, toks)
    dma = pltpu.SemaphoreType.DMA
    scratch = [
        vm((width, toks), BF16), vm(slots, BF16), vm((8, 128), jnp.int32), vm((NS, 8, 128), jnp.int32),
        vm((width, frames), BF16), vm((width, frames), BF16),
        vm((heads, frames, HD), BF16), vm((heads, frames, HD), BF16),
        vm((NS + 1, heads, frames, toks), F32),
        vm((width, toks), F32), vm(rows8, F32),
        vm(slots, BF16), vm((NS,) + rows8, F32), vm(slots, BF16), vm((NS,) + rows8, F32),
        vm((width, toks), F32), vm((width, toks), F32), vm((width, toks), BF16),
        vm(rows8, F32), vm((NS,) + rows8, F32), vm(slots, BF16), vm((NS,) + rows8, F32),
        vm((width, toks), F32), vm(slots, BF16), vm(slots, BF16),
        vm((width, frames), F32), vm((width, frames), F32),
        vm((2 * n_t + 1, 16, toks), F32), vm((2 * n_g + 1, 8, width), F32),
        vm((width, toks), F32),
        dma((NS, groups)), dma((NS, groups)), dma((NS,)), dma((NS,)),
    ] + [dma((NS, groups)) for _ in range(10)] + [
        dma((n_t,)), dma((n_t,)), dma((n_g,)), dma((n_g,)),
    ]
    vspec = pl.BlockSpec(memory_space=pltpu.VMEM)
    sspec = pl.BlockSpec(memory_space=pltpu.SMEM)
    outs = pl.pallas_call(
        functools.partial(body, sizes),
        out_shape=(
            jax.ShapeDtypeStruct((toks, width), BF16),
            jax.ShapeDtypeStruct((toks, width), BF16),
            jax.ShapeDtypeStruct((frames, width), BF16),
            jax.ShapeDtypeStruct((frames, width), BF16),
            jax.ShapeDtypeStruct((1, width), F32),
        ),
        in_specs=[vspec] * 5 + [sspec] * 2,
        out_specs=(vspec,) * 5,
        scratch_shapes=scratch,
        compiler_params=pltpu.CompilerParams(
            collective_id=0, has_side_effects=True, vmem_limit_bytes=58 * 1024 * 1024
        ),
    )(queries[0], keys[0], values[0], grad_out[0], gain[None], band_start[0], band_end[0])
    attended, grad_q, grad_k, grad_v, grad_gain = outs
    return attended[None], grad_q[None], grad_k[None], grad_v[None], grad_gain[0]


def solution(mesh):
    sizes = (mesh.shape["dp"], mesh.shape["seq"], mesh.shape["tensor"])
    return jax.shard_map(
        functools.partial(per_device, sizes),
        mesh=mesh,
        in_specs=(
            P("dp", "seq", "tensor"),
            P("dp", "seq", "tensor"),
            P("dp", "seq", "tensor"),
            P("dp", "seq", "tensor"),
            P("tensor"),
            P("dp", "seq"),
            P("dp", "seq"),
        ),
        out_specs=(
            P("dp", "seq", "tensor"),
            P("dp", "seq", "tensor"),
            P("dp", "seq", "tensor"),
            P("dp", "seq", "tensor"),
            P("tensor"),
        ),
        check_vma=False,
    )
```

```python
import functools

import jax
import jax.numpy as jnp
from jax import lax
from jax.experimental import pallas as pl
from jax.experimental.pallas import tpu as pltpu
from jax.sharding import PartitionSpec as P

D = 3072
HD = 96
EB = 128
GH = 4
GW = GH * HD
OFFS = (-1, 1, -2, 2)
NS = len(OFFS)
OWN = NS
NEG = -1e30
EPS = 1e-06
MESH = pl.DeviceIdType.MESH
F32 = jnp.float32
BF16 = jnp.bfloat16


def dot_nn(a, b):
    return jnp.dot(a, b, preferred_element_type=F32)


def dot_nt(a, b):
    return lax.dot_general(a, b, (((1,), (1,)), ((), ())), preferred_element_type=F32)


def xor_strides(size):
    out = []
    s = 1
    while s < size:
        out.append(s)
        s *= 2
    return out


def xor_partner(index, stride):
    return index + stride - 2 * stride * ((index // stride) % 2)


def body(
    sizes, q_ref, k_ref, v_ref, g_ref, gain_ref, bs_ref, be_ref,
    att_ref, dq_ref, dk_ref, dv_ref, dg_ref,
    qt, qin, band, bandin, kt, vt, kh, vh, e, oown, sown, oout, sout, oin, sin,
    attn, sgt, dot, cown, cout, doin, cin, dqown, dqout, dqin, dkt, dvt, stat, gg, norm,
    q_s, q_r, b_s, b_r, o_s, o_r, s_s, s_r, d_s, d_r, c_s, c_r, x_s, x_r,
    t_s, t_r, gg_s, gg_r, qf_s, df_s,
):
    n_dp, n_seq, n_tensor = sizes
    toks, width = q_ref.shape
    frames = k_ref.shape[0]
    groups = width // GW
    scale = HD ** (-0.5)
    me = lax.axis_index("seq")
    tp = lax.axis_index("tensor")
    dp = lax.axis_index("dp")

    def inside(i):
        return (i >= 0) & (i < n_seq)

    barrier = pltpu.get_barrier_semaphore()
    t_strides = xor_strides(n_tensor)
    gain_stages = [("seq", s) for s in xor_strides(n_seq)] + [("dp", s) for s in xor_strides(n_dp)]
    for i, d in enumerate(OFFS):
        @pl.when(inside(me + d))
        def _(d=d):
            pl.semaphore_signal(barrier, inc=1, device_id={"seq": me + d}, device_id_type=MESH)
    fixed = 0
    for s in t_strides:
        pl.semaphore_signal(barrier, inc=1, device_id={"tensor": xor_partner(tp, s)}, device_id_type=MESH)
        fixed += 1
    for axis, s in gain_stages:
        if axis == "seq" and s > 2:
            pl.semaphore_signal(barrier, inc=1, device_id={"seq": xor_partner(me, s)}, device_id_type=MESH)
            fixed += 1
        if axis == "dp":
            pl.semaphore_signal(barrier, inc=1, device_id={"dp": xor_partner(dp, s)}, device_id_type=MESH)
            fixed += 1

    band[0:4, :] = jnp.full((4, 128), bs_ref[0], jnp.int32)
    band[4:8, :] = jnp.full((4, 128), be_ref[0], jnp.int32)

    def tcols(c):
        return pl.ds(pl.multiple_of(c * 128, 128), 128)

    def q_body(c, _):
        qt[tcols(c), :] = q_ref[:, tcols(c)].T
        return 0
    lax.fori_loop(0, width // 128, q_body, 0, unroll=3)

    peers = jnp.int32(fixed)
    for d in OFFS:
        peers = peers + jnp.where(inside(me + d), 1, 0).astype(jnp.int32)
    pl.semaphore_wait(barrier, peers)

    def rows(g):
        return pl.ds(pl.multiple_of(g * GW, GW), GW)

    def hrows(g, j):
        return pl.ds(pl.multiple_of(g * GW + j * HD, 32), HD)

    def remote(src, dst, ss, rs, to):
        return pltpu.make_async_remote_copy(
            src_ref=src, dst_ref=dst, send_sem=ss, recv_sem=rs,
            device_id={"seq": to}, device_id_type=MESH,
        )

    def q_copy(i, g):
        return remote(qt.at[rows(g)], qin.at[i, rows(g)], q_s.at[i, g], q_r.at[i, g], me + OFFS[i])

    def b_copy(i):
        return remote(band, bandin.at[i], b_s.at[i], b_r.at[i], me + OFFS[i])

    def o_copy(i, g):
        return remote(oout.at[i, rows(g)], oin.at[i, rows(g)], o_s.at[i, g], o_r.at[i, g], me - OFFS[i])

    def s_copy(i, g):
        return remote(sout.at[i, g], sin.at[i, g], s_s.at[i, g], s_r.at[i, g], me - OFFS[i])

    def d_copy(i, g):
        return remote(dot.at[rows(g)], doin.at[i, rows(g)], d_s.at[i, g], d_r.at[i, g], me + OFFS[i])

    def c_copy(i, g):
        return remote(cout.at[i, g], cin.at[i, g], c_s.at[i, g], c_r.at[i, g], me + OFFS[i])

    def x_copy(i, g):
        return remote(dqout.at[i, rows(g)], dqin.at[i, rows(g)], x_s.at[i, g], x_r.at[i, g], me - OFFS[i])

    def to_target(i):
        return pl.when(inside(me + OFFS[i]))

    def to_client(i):
        return pl.when(inside(me - OFFS[i]))

    odd = lax.rem(me, 2) == 1

    def direct(i):
        ok = inside(me + OFFS[i])
        if i >= 2:
            ok = ok & (odd if OFFS[i] < 0 else jnp.logical_not(odd))
        return pl.when(ok)

    def relays(i):
        return pl.when(inside(me - OFFS[i]) & (odd if OFFS[i] < 0 else jnp.logical_not(odd)))

    def qf_copy(i, g):
        return remote(qin.at[i, rows(g)], qin.at[i + 2, rows(g)], qf_s.at[g], q_r.at[i + 2, g], me + OFFS[i])

    def df_copy(i, g):
        return remote(doin.at[i, rows(g)], doin.at[i + 2, rows(g)], df_s.at[g], d_r.at[i + 2, g], me + OFFS[i])

    for i in range(NS):
        @to_target(i)
        def _(i=i):
            b_copy(i).start()

    def q_send(g, _):
        for i in range(NS):
            @direct(i)
            def _(i=i):
                q_copy(i, g).start()
        return 0
    lax.fori_loop(0, groups, q_send, 0)

    def v_body(c, _):
        vt[tcols(c), :] = v_ref[:, tcols(c)].T
        return 0
    lax.fori_loop(0, width // 128, v_body, 0, unroll=3)

    def split_heads(src, dst):
        def head_body(g, _):
            x = src[:, rows(g)]
            for j in range(GH):
                dst[g * GH + j] = x[:, j * HD:(j + 1) * HD]
            return 0
        lax.fori_loop(0, groups, head_body, 0)
    split_heads(k_ref, kh)

    def forward(g, q_at, band_at, slot, o_put, s_put):
        start = band_at[0:1, :]
        end = band_at[4:5, :]
        first = me * (frames // EB)
        bias = []
        for b in range(frames // EB):
            ok = (first + b >= start) & (first + b < end)
            bias.append(jnp.where(ok, 0.0, NEG).astype(F32))
        for j in range(GH):
            h = g * GH + j
            s = dot_nn(kh[h], q_at[hrows(g, j), :]) * scale
            s = jnp.concatenate([s[b * EB:(b + 1) * EB] + bias[b] for b in range(frames // EB)], axis=0)
            top = jnp.max(s, axis=0, keepdims=True)
            w = jnp.exp(s - top)
            e[slot, h] = w
            s_put(g, j, top, jnp.sum(w, axis=0, keepdims=True))
            o_put(g, j, dot_nn(vt[hrows(g, j), :], w.astype(BF16)))

    def own_fwd(g, _):
        def o_put(g, j, o):
            oown[hrows(g, j), :] = o

        def s_put(g, j, top, total):
            sown[g, j:j + 1, :] = top
            sown[g, GH + j:GH + j + 1, :] = total
        forward(g, qt, band, OWN, o_put, s_put)
        return 0
    lax.fori_loop(0, groups, own_fwd, 0)

    for i in range(NS):
        @pl.when(jnp.logical_not(inside(me + OFFS[i])))
        def _(i=i):
            oin[i] = jnp.zeros(oin.shape[1:], BF16)
            sin[i, :, 0:GH, :] = jnp.full((groups, GH, toks), NEG, F32)
            sin[i, :, GH:, :] = jnp.zeros((groups, GH, toks), F32)
            dqin[i] = jnp.zeros(dqin.shape[1:], BF16)

    for i in range(NS):
        @to_client(i)
        def _(i=i):
            b_copy(i).wait_recv()

    def serve_fwd(g, _):
        for i in range(2):
            @to_client(i)
            def _(i=i):
                q_copy(i, g).wait_recv()

            @relays(i)
            def _(i=i):
                qf_copy(i, g).start()
        for i in range(NS):
            @to_client(i)
            def _(i=i):
                if i >= 2:
                    q_copy(i, g).wait_recv()

                def o_put(g, j, o):
                    oout[i, hrows(g, j), :] = o.astype(BF16)

                def s_put(g, j, top, total):
                    sout[i, g, j:j + 1, :] = top
                    sout[i, g, GH + j:GH + j + 1, :] = total
                forward(g, qin.at[i], bandin.at[i], i, o_put, s_put)
                s_copy(i, g).start()
                o_copy(i, g).start()
        return 0
    lax.fori_loop(0, groups, serve_fwd, 0)

    def k_body(c, _):
        kt[tcols(c), :] = k_ref[:, tcols(c)].T
        sgt[tcols(c), :] = (g_ref[:, tcols(c)].astype(F32) * gain_ref[:, tcols(c)]).T
        return 0
    lax.fori_loop(0, width // 128, k_body, 0, unroll=3)
    split_heads(v_ref, vh)

    def fold(x):
        return jnp.sum(x.reshape(x.shape[0] // 8, 8, x.shape[1]), axis=0)

    def combine(g, carry):
        square, cross = carry
        for i in range(NS):
            @to_target(i)
            def _(i=i):
                s_copy(i, g).wait_recv()
                o_copy(i, g).wait_recv()
        for j in range(GH):
            tops = [sin[i, g, j:j + 1, :] for i in range(NS)] + [sown[g, j:j + 1, :]]
            sums = [sin[i, g, GH + j:GH + j + 1, :] for i in range(NS)] + [sown[g, GH + j:GH + j + 1, :]]
            top = functools.reduce(jnp.maximum, tops)
            ws = [jnp.exp(t - top) for t in tops]
            total = functools.reduce(lambda a, b: a + b, [w * x for w, x in zip(ws, sums)])
            inv = 1.0 / total
            cs = [w * inv for w in ws]
            acc = oown[hrows(g, j), :] * cs[OWN]
            for i in range(NS):
                acc = acc + oin[i, hrows(g, j), :].astype(F32) * cs[i]
                cout[i, g, j:j + 1, :] = cs[i]
            cown[g, j:j + 1, :] = cs[OWN]
            attn[hrows(g, j), :] = acc
            square = square + fold(acc * acc)
            cross = cross + fold(acc * sgt[hrows(g, j), :])
        return square, cross
    zero = jnp.zeros((8, toks), F32)
    square, cross = lax.fori_loop(0, groups, combine, (zero, zero))

    stat[0, 0:8, :] = square
    stat[0, 8:16, :] = cross
    for number, s in enumerate(t_strides):
        copy = pltpu.make_async_remote_copy(
            src_ref=stat.at[2 * number], dst_ref=stat.at[2 * number + 1],
            send_sem=t_s.at[number], recv_sem=t_r.at[number],
            device_id={"tensor": xor_partner(tp, s)}, device_id_type=MESH,
        )
        copy.start()
        copy.wait()
        stat[2 * number + 2] = stat[2 * number] + stat[2 * number + 1]
    last = 2 * len(t_strides)
    square = jnp.sum(stat[last, 0:8, :], axis=0, keepdims=True)
    cross = jnp.sum(stat[last, 8:16, :], axis=0, keepdims=True)
    inv_rms = lax.rsqrt(square / D + EPS)
    mean_cross = inv_rms * cross / D

    def grad_attn(g, _):
        for j in range(GH):
            a = attn[hrows(g, j), :]
            normed = a * inv_rms
            norm[hrows(g, j), :] = normed
            da = (inv_rms * (sgt[hrows(g, j), :] - normed * mean_cross)).astype(BF16)
            dot[hrows(g, j), :] = da
            inner = jnp.sum(da.astype(F32) * a, axis=0, keepdims=True)
            cown[g, GH + j:GH + j + 1, :] = inner
            for i in range(NS):
                cout[i, g, GH + j:GH + j + 1, :] = inner
        for i in range(NS):
            @to_target(i)
            def _(i=i):
                c_copy(i, g).start()

            @direct(i)
            def _(i=i):
                d_copy(i, g).start()
        return 0
    lax.fori_loop(0, groups, grad_attn, 0)

    def att_body(c, _):
        normed = norm[tcols(c), :].T
        att_ref[:, tcols(c)] = (normed * gain_ref[:, tcols(c)]).astype(BF16)
        gg[0, :, tcols(c)] = fold(normed * g_ref[:, tcols(c)].astype(F32))
        return 0
    lax.fori_loop(0, width // 128, att_body, 0, unroll=3)

    def gain_copy(number):
        axis, s = gain_stages[number]
        index = me if axis == "seq" else dp
        return pltpu.make_async_remote_copy(
            src_ref=gg.at[2 * number], dst_ref=gg.at[2 * number + 1],
            send_sem=gg_s.at[number], recv_sem=gg_r.at[number],
            device_id={axis: xor_partner(index, s)}, device_id_type=MESH,
        )

    def gain_finish(number):
        gain_copy(number).wait()
        gg[2 * number + 2] = gg[2 * number] + gg[2 * number + 1]

    def backward(g, q_at, d_at, c_at, slot, dq_put, first):
        for j in range(GH):
            h = g * GH + j
            q = q_at[hrows(g, j), :]
            da = d_at[hrows(g, j), :]
            p = e[slot, h] * c_at[g, j:j + 1, :]
            pb = p.astype(BF16)
            dp_ = dot_nn(vh[h], da)
            ds = (p * (dp_ - c_at[g, GH + j:GH + j + 1, :])).astype(BF16)
            dk = dot_nt(q, ds)
            dv = dot_nt(da, pb)
            if first:
                dkt[hrows(g, j), :] = dk
                dvt[hrows(g, j), :] = dv
            else:
                dkt[hrows(g, j), :] += dk
                dvt[hrows(g, j), :] += dv
            dq_put(g, j, dot_nn(kt[hrows(g, j), :], ds) * scale)

    def own_put(g, j, x):
        dqown[hrows(g, j), :] = x

    stages = len(gain_stages)
    gain_copy(0).start()
    for g in range(groups):
        backward(g, qt, dot, cown, OWN, own_put, True)
        if g < stages:
            gain_finish(g)
            if g + 1 < stages:
                gain_copy(g + 1).start()

    def serve_bwd(g, _):
        for i in range(2):
            @to_client(i)
            def _(i=i):
                d_copy(i, g).wait_recv()

            @relays(i)
            def _(i=i):
                df_copy(i, g).start()
        for i in range(NS):
            @to_client(i)
            def _(i=i):
                c_copy(i, g).wait_recv()
                if i >= 2:
                    d_copy(i, g).wait_recv()

                def put(g, j, x):
                    dqout[i, hrows(g, j), :] = x.astype(BF16)
                backward(g, qin.at[i], doin.at[i], cin.at[i], i, put, False)
                x_copy(i, g).start()
        return 0
    lax.fori_loop(0, groups, serve_bwd, 0)

    for number in range(groups, stages):
        gain_finish(number)
        if number + 1 < stages:
            gain_copy(number + 1).start()
    dg_ref[...] = jnp.sum(gg[2 * stages], axis=0, keepdims=True)

    def out_kv(c, _):
        dk_ref[:, tcols(c)] = (dkt[tcols(c), :] * scale).astype(BF16).T
        dv_ref[:, tcols(c)] = dvt[tcols(c), :].astype(BF16).T
        return 0
    lax.fori_loop(0, width // 128, out_kv, 0, unroll=3)

    def out_q(g, _):
        for i in range(NS):
            @to_target(i)
            def _(i=i):
                x_copy(i, g).wait_recv()
        for c in range(GW // 128):
            at = tcols(g * (GW // 128) + c)
            acc = dqown[at, :]
            for i in range(NS):
                acc = acc + dqin[i, at, :].astype(F32)
            dq_ref[:, at] = acc.astype(BF16).T
        return 0
    lax.fori_loop(0, groups, out_q, 0)

    def drain(g, _):
        for i in range(NS):
            @to_target(i)
            def _(i=i):
                c_copy(i, g).wait_send()

            @direct(i)
            def _(i=i):
                q_copy(i, g).wait_send()
                d_copy(i, g).wait_send()
            if i < 2:
                @relays(i)
                def _(i=i):
                    qf_copy(i, g).wait_send()
                    df_copy(i, g).wait_send()

            @to_client(i)
            def _(i=i):
                o_copy(i, g).wait_send()
                s_copy(i, g).wait_send()
                x_copy(i, g).wait_send()
        return 0
    lax.fori_loop(0, groups, drain, 0)
    for i in range(NS):
        @to_target(i)
        def _(i=i):
            b_copy(i).wait_send()


def per_device(sizes, queries, keys, values, grad_out, gain, band_start, band_end):
    toks, width = queries.shape[1:]
    frames = keys.shape[1]
    heads = width // HD
    groups = width // GW
    n_dp, n_seq, n_tensor = sizes
    n_t = len(xor_strides(n_tensor))
    n_g = len(xor_strides(n_seq)) + len(xor_strides(n_dp))
    vm = pltpu.VMEM
    slots = (NS, width, toks)
    rows8 = (groups, 8, toks)
    dma = pltpu.SemaphoreType.DMA
    scratch = [
        vm((width, toks), BF16), vm(slots, BF16), vm((8, 128), jnp.int32), vm((NS, 8, 128), jnp.int32),
        vm((width, frames), BF16), vm((width, frames), BF16),
        vm((heads, frames, HD), BF16), vm((heads, frames, HD), BF16),
        vm((NS + 1, heads, frames, toks), F32),
        vm((width, toks), F32), vm(rows8, F32),
        vm(slots, BF16), vm((NS,) + rows8, F32), vm(slots, BF16), vm((NS,) + rows8, F32),
        vm((width, toks), F32), vm((width, toks), F32), vm((width, toks), BF16),
        vm(rows8, F32), vm((NS,) + rows8, F32), vm(slots, BF16), vm((NS,) + rows8, F32),
        vm((width, toks), F32), vm(slots, BF16), vm(slots, BF16),
        vm((width, frames), F32), vm((width, frames), F32),
        vm((2 * n_t + 1, 16, toks), F32), vm((2 * n_g + 1, 8, width), F32),
        vm((width, toks), F32),
        dma((NS, groups)), dma((NS, groups)), dma((NS,)), dma((NS,)),
    ] + [dma((NS, groups)) for _ in range(10)] + [
        dma((n_t,)), dma((n_t,)), dma((n_g,)), dma((n_g,)), dma((groups,)), dma((groups,)),
    ]
    vspec = pl.BlockSpec(memory_space=pltpu.VMEM)
    sspec = pl.BlockSpec(memory_space=pltpu.SMEM)
    outs = pl.pallas_call(
        functools.partial(body, sizes),
        out_shape=(
            jax.ShapeDtypeStruct((toks, width), BF16),
            jax.ShapeDtypeStruct((toks, width), BF16),
            jax.ShapeDtypeStruct((frames, width), BF16),
            jax.ShapeDtypeStruct((frames, width), BF16),
            jax.ShapeDtypeStruct((1, width), F32),
        ),
        in_specs=[vspec] * 5 + [sspec] * 2,
        out_specs=(vspec,) * 5,
        scratch_shapes=scratch,
        compiler_params=pltpu.CompilerParams(
            collective_id=0, has_side_effects=True, vmem_limit_bytes=58 * 1024 * 1024
        ),
    )(queries[0], keys[0], values[0], grad_out[0], gain[None], band_start[0], band_end[0])
    attended, grad_q, grad_k, grad_v, grad_gain = outs
    return attended[None], grad_q[None], grad_k[None], grad_v[None], grad_gain[0]


def solution(mesh):
    sizes = (mesh.shape["dp"], mesh.shape["seq"], mesh.shape["tensor"])
    return jax.shard_map(
        functools.partial(per_device, sizes),
        mesh=mesh,
        in_specs=(
            P("dp", "seq", "tensor"),
            P("dp", "seq", "tensor"),
            P("dp", "seq", "tensor"),
            P("dp", "seq", "tensor"),
            P("tensor"),
            P("dp", "seq"),
            P("dp", "seq"),
        ),
        out_specs=(
            P("dp", "seq", "tensor"),
            P("dp", "seq", "tensor"),
            P("dp", "seq", "tensor"),
            P("dp", "seq", "tensor"),
            P("tensor"),
        ),
        check_vma=False,
    )
```

```python
import functools

import jax
import jax.numpy as jnp
from jax import lax
from jax.experimental import pallas as pl
from jax.experimental.pallas import tpu as pltpu
from jax.sharding import PartitionSpec as P

D = 3072
HD = 96
EB = 128
GH = 4
GW = GH * HD
OFFS = (-1, 1, -2, 2)
NS = len(OFFS)
OWN = NS
NEG = -1e30
EPS = 1e-06
MESH = pl.DeviceIdType.MESH
F32 = jnp.float32
BF16 = jnp.bfloat16


def dot_nn(a, b):
    return jnp.dot(a, b, preferred_element_type=F32)


def dot_nt(a, b):
    return lax.dot_general(a, b, (((1,), (1,)), ((), ())), preferred_element_type=F32)


def xor_strides(size):
    out = []
    s = 1
    while s < size:
        out.append(s)
        s *= 2
    return out


def xor_partner(index, stride):
    return index + stride - 2 * stride * ((index // stride) % 2)


def body(
    sizes, q_ref, k_ref, v_ref, g_ref, gain_ref, bs_ref, be_ref,
    att_ref, dq_ref, dk_ref, dv_ref, dg_ref,
    qt, qin, band, bandin, kt, vt, kh, vh, e, oown, sown, oout, sout, oin, sin,
    attn, sgt, dot, cown, cout, doin, cin, dqown, dqout, dqin, dkt, dvt, stat, gg, norm,
    q_s, q_r, b_s, b_r, o_s, o_r, s_s, s_r, d_s, d_r, c_s, c_r, x_s, x_r,
    t_s, t_r, gg_s, gg_r, qf_s, df_s,
    omate, smate, dqmate, om_s, om_r, sm_s, sm_r, xm_s, xm_r,
):
    n_dp, n_seq, n_tensor = sizes
    toks, width = q_ref.shape
    frames = k_ref.shape[0]
    groups = width // GW
    scale = HD ** (-0.5)
    me = lax.axis_index("seq")
    tp = lax.axis_index("tensor")
    dp = lax.axis_index("dp")

    def inside(i):
        return (i >= 0) & (i < n_seq)

    barrier = pltpu.get_barrier_semaphore()
    t_strides = xor_strides(n_tensor)
    gain_stages = [("seq", s) for s in xor_strides(n_seq)] + [("dp", s) for s in xor_strides(n_dp)]
    for i, d in enumerate(OFFS):
        @pl.when(inside(me + d))
        def _(d=d):
            pl.semaphore_signal(barrier, inc=1, device_id={"seq": me + d}, device_id_type=MESH)
    fixed = 0
    for s in t_strides:
        pl.semaphore_signal(barrier, inc=1, device_id={"tensor": xor_partner(tp, s)}, device_id_type=MESH)
        fixed += 1
    for axis, s in gain_stages:
        if axis == "seq" and s > 2:
            pl.semaphore_signal(barrier, inc=1, device_id={"seq": xor_partner(me, s)}, device_id_type=MESH)
            fixed += 1
        if axis == "dp":
            pl.semaphore_signal(barrier, inc=1, device_id={"dp": xor_partner(dp, s)}, device_id_type=MESH)
            fixed += 1

    band[0:4, :] = jnp.full((4, 128), bs_ref[0], jnp.int32)
    band[4:8, :] = jnp.full((4, 128), be_ref[0], jnp.int32)

    def tcols(c):
        return pl.ds(pl.multiple_of(c * 128, 128), 128)

    def q_body(c, _):
        qt[tcols(c), :] = q_ref[:, tcols(c)].T
        return 0
    lax.fori_loop(0, width // 128, q_body, 0, unroll=3)

    peers = jnp.int32(fixed)
    for d in OFFS:
        peers = peers + jnp.where(inside(me + d), 1, 0).astype(jnp.int32)
    pl.semaphore_wait(barrier, peers)

    def rows(g):
        return pl.ds(pl.multiple_of(g * GW, GW), GW)

    def hrows(g, j):
        return pl.ds(pl.multiple_of(g * GW + j * HD, 32), HD)

    def remote(src, dst, ss, rs, to):
        return pltpu.make_async_remote_copy(
            src_ref=src, dst_ref=dst, send_sem=ss, recv_sem=rs,
            device_id={"seq": to}, device_id_type=MESH,
        )

    def q_copy(i, g):
        return remote(qt.at[rows(g)], qin.at[i, rows(g)], q_s.at[i, g], q_r.at[i, g], me + OFFS[i])

    def b_copy(i):
        return remote(band, bandin.at[i], b_s.at[i], b_r.at[i], me + OFFS[i])

    def o_copy(i, g):
        return remote(oout.at[i, rows(g)], oin.at[i, rows(g)], o_s.at[i, g], o_r.at[i, g], me - OFFS[i])

    def s_copy(i, g):
        return remote(sout.at[i, g], sin.at[i, g], s_s.at[i, g], s_r.at[i, g], me - OFFS[i])

    def d_copy(i, g):
        return remote(dot.at[rows(g)], doin.at[i, rows(g)], d_s.at[i, g], d_r.at[i, g], me + OFFS[i])

    def c_copy(i, g):
        return remote(cout.at[i, g], cin.at[i, g], c_s.at[i, g], c_r.at[i, g], me + OFFS[i])

    def x_copy(i, g):
        return remote(dqout.at[i, rows(g)], dqin.at[i, rows(g)], x_s.at[i, g], x_r.at[i, g], me - OFFS[i])

    def to_target(i):
        return pl.when(inside(me + OFFS[i]))

    def to_client(i):
        return pl.when(inside(me - OFFS[i]))

    odd = lax.rem(me, 2) == 1

    def direct(i):
        ok = inside(me + OFFS[i])
        if i >= 2:
            ok = ok & (odd if OFFS[i] < 0 else jnp.logical_not(odd))
        return pl.when(ok)

    def relays(i):
        return pl.when(inside(me - OFFS[i]) & (odd if OFFS[i] < 0 else jnp.logical_not(odd)))

    def mated(i):
        return pl.when(inside(me - OFFS[i]) & (jnp.logical_not(odd) if OFFS[i] < 0 else odd))

    def unmated(i):
        ok = inside(me - OFFS[i])
        if i >= 2:
            ok = ok & (odd if OFFS[i] < 0 else jnp.logical_not(odd))
        return pl.when(ok)

    def om_copy(i, g):
        return remote(oout.at[i, rows(g)], omate.at[rows(g)], om_s.at[g], om_r.at[g], me - OFFS[i - 2])

    def sm_copy(i, g):
        return remote(sout.at[i, g], smate.at[g], sm_s.at[g], sm_r.at[g], me - OFFS[i - 2])

    def xm_copy(i, g):
        return remote(dqout.at[i, rows(g)], dqmate.at[rows(g)], xm_s.at[g], xm_r.at[g], me - OFFS[i - 2])

    def qf_copy(i, g):
        return remote(qin.at[i, rows(g)], qin.at[i + 2, rows(g)], qf_s.at[g], q_r.at[i + 2, g], me + OFFS[i])

    def df_copy(i, g):
        return remote(doin.at[i, rows(g)], doin.at[i + 2, rows(g)], df_s.at[g], d_r.at[i + 2, g], me + OFFS[i])

    for i in range(NS):
        @to_target(i)
        def _(i=i):
            b_copy(i).start()

    def q_send(g, _):
        for i in range(NS):
            @direct(i)
            def _(i=i):
                q_copy(i, g).start()
        return 0
    lax.fori_loop(0, groups, q_send, 0)

    def v_body(c, _):
        vt[tcols(c), :] = v_ref[:, tcols(c)].T
        return 0
    lax.fori_loop(0, width // 128, v_body, 0, unroll=3)

    def split_heads(src, dst):
        def head_body(g, _):
            x = src[:, rows(g)]
            for j in range(GH):
                dst[g * GH + j] = x[:, j * HD:(j + 1) * HD]
            return 0
        lax.fori_loop(0, groups, head_body, 0)
    split_heads(k_ref, kh)

    def forward(g, q_at, band_at, slot, o_put, s_put):
        start = band_at[0:1, :]
        end = band_at[4:5, :]
        first = me * (frames // EB)
        bias = []
        for b in range(frames // EB):
            ok = (first + b >= start) & (first + b < end)
            bias.append(jnp.where(ok, 0.0, NEG).astype(F32))
        for j in range(GH):
            h = g * GH + j
            s = dot_nn(kh[h], q_at[hrows(g, j), :]) * scale
            s = jnp.concatenate([s[b * EB:(b + 1) * EB] + bias[b] for b in range(frames // EB)], axis=0)
            top = jnp.max(s, axis=0, keepdims=True)
            w = jnp.exp(s - top)
            e[slot, h] = w
            s_put(g, j, top, jnp.sum(w, axis=0, keepdims=True))
            o_put(g, j, dot_nn(vt[hrows(g, j), :], w.astype(BF16)))

    def own_fwd(g, _):
        def o_put(g, j, o):
            oown[hrows(g, j), :] = o

        def s_put(g, j, top, total):
            sown[g, j:j + 1, :] = top
            sown[g, GH + j:GH + j + 1, :] = total
        forward(g, qt, band, OWN, o_put, s_put)
        return 0
    lax.fori_loop(0, groups, own_fwd, 0)

    for i in range(NS):
        there = inside(me + OFFS[i])
        replies = there
        if i >= 2:
            replies = there & (odd if OFFS[i] < 0 else jnp.logical_not(odd))

        @pl.when(jnp.logical_not(there))
        def _(i=i):
            sin[i, :, 0:GH, :] = jnp.full((groups, GH, toks), NEG, F32)
            sin[i, :, GH:, :] = jnp.zeros((groups, GH, toks), F32)

        @pl.when(jnp.logical_not(replies))
        def _(i=i):
            oin[i] = jnp.zeros(oin.shape[1:], BF16)
            dqin[i] = jnp.zeros(dqin.shape[1:], BF16)

    for i in range(NS):
        @to_client(i)
        def _(i=i):
            b_copy(i).wait_recv()

    def serve_fwd(g, _):
        for i in range(2):
            @to_client(i)
            def _(i=i):
                q_copy(i, g).wait_recv()

            @relays(i)
            def _(i=i):
                qf_copy(i, g).start()
        for i in (2, 3, 0, 1):
            @to_client(i)
            def _(i=i):
                if i >= 2:
                    q_copy(i, g).wait_recv()

                def o_put(g, j, o):
                    oout[i, hrows(g, j), :] = o.astype(BF16)

                def s_put(g, j, top, total):
                    sout[i, g, j:j + 1, :] = top
                    sout[i, g, GH + j:GH + j + 1, :] = total
                forward(g, qin.at[i], bandin.at[i], i, o_put, s_put)
                s_copy(i, g).start()
            if i >= 2:
                @mated(i)
                def _(i=i):
                    sm_copy(i, g).start()
                    om_copy(i, g).start()
            else:
                @relays(i)
                def _(i=i):
                    sm_copy(i + 2, g).wait_recv()
                    om_copy(i + 2, g).wait_recv()
                    for j in range(GH):
                        a = sout[i, g, j:j + 1, :]
                        b = smate[g, j:j + 1, :]
                        top = jnp.maximum(a, b)
                        both = (oout[i, hrows(g, j), :].astype(F32) * jnp.exp(a - top)
                                + omate[hrows(g, j), :].astype(F32) * jnp.exp(b - top))
                        oout[i, hrows(g, j), :] = both.astype(BF16)

            @unmated(i)
            def _(i=i):
                o_copy(i, g).start()
        return 0
    lax.fori_loop(0, groups, serve_fwd, 0)

    def k_body(c, _):
        kt[tcols(c), :] = k_ref[:, tcols(c)].T
        sgt[tcols(c), :] = (g_ref[:, tcols(c)].astype(F32) * gain_ref[:, tcols(c)]).T
        return 0
    lax.fori_loop(0, width // 128, k_body, 0, unroll=3)
    split_heads(v_ref, vh)

    def fold(x):
        return jnp.sum(x.reshape(x.shape[0] // 8, 8, x.shape[1]), axis=0)

    lone = [jnp.where(odd if OFFS[i] > 0 else jnp.logical_not(odd), 0.0, NEG).astype(F32) for i in range(2)]

    def combine(g, carry):
        square, cross = carry
        for i in range(NS):
            @to_target(i)
            def _(i=i):
                s_copy(i, g).wait_recv()

            @direct(i)
            def _(i=i):
                o_copy(i, g).wait_recv()
        for j in range(GH):
            tops = [sin[i, g, j:j + 1, :] for i in range(NS)] + [sown[g, j:j + 1, :]]
            sums = [sin[i, g, GH + j:GH + j + 1, :] for i in range(NS)] + [sown[g, GH + j:GH + j + 1, :]]
            top = functools.reduce(jnp.maximum, tops)
            ws = [jnp.exp(t - top) for t in tops]
            total = functools.reduce(lambda a, b: a + b, [w * x for w, x in zip(ws, sums)])
            inv = 1.0 / total
            cs = [w * inv for w in ws]
            acc = oown[hrows(g, j), :] * cs[OWN]
            for i in range(NS):
                co = cs[i] if i >= 2 else jnp.exp(jnp.maximum(tops[i], tops[i + 2] + lone[i]) - top) * inv
                acc = acc + oin[i, hrows(g, j), :].astype(F32) * co
                cout[i, g, j:j + 1, :] = cs[i]
            cown[g, j:j + 1, :] = cs[OWN]
            attn[hrows(g, j), :] = acc
            square = square + fold(acc * acc)
            cross = cross + fold(acc * sgt[hrows(g, j), :])
        return square, cross
    zero = jnp.zeros((8, toks), F32)
    square, cross = lax.fori_loop(0, groups, combine, (zero, zero))

    stat[0, 0:8, :] = square
    stat[0, 8:16, :] = cross
    for number, s in enumerate(t_strides):
        copy = pltpu.make_async_remote_copy(
            src_ref=stat.at[2 * number], dst_ref=stat.at[2 * number + 1],
            send_sem=t_s.at[number], recv_sem=t_r.at[number],
            device_id={"tensor": xor_partner(tp, s)}, device_id_type=MESH,
        )
        copy.start()
        copy.wait()
        stat[2 * number + 2] = stat[2 * number] + stat[2 * number + 1]
    last = 2 * len(t_strides)
    square = jnp.sum(stat[last, 0:8, :], axis=0, keepdims=True)
    cross = jnp.sum(stat[last, 8:16, :], axis=0, keepdims=True)
    inv_rms = lax.rsqrt(square / D + EPS)
    mean_cross = inv_rms * cross / D

    def grad_attn(g, _):
        for j in range(GH):
            a = attn[hrows(g, j), :]
            normed = a * inv_rms
            norm[hrows(g, j), :] = normed
            da = (inv_rms * (sgt[hrows(g, j), :] - normed * mean_cross)).astype(BF16)
            dot[hrows(g, j), :] = da
            inner = jnp.sum(da.astype(F32) * a, axis=0, keepdims=True)
            cown[g, GH + j:GH + j + 1, :] = inner
            for i in range(NS):
                cout[i, g, GH + j:GH + j + 1, :] = inner
        for i in range(NS):
            @to_target(i)
            def _(i=i):
                c_copy(i, g).start()

            @direct(i)
            def _(i=i):
                d_copy(i, g).start()
        return 0
    lax.fori_loop(0, groups, grad_attn, 0)

    def att_body(c, _):
        normed = norm[tcols(c), :].T
        att_ref[:, tcols(c)] = (normed * gain_ref[:, tcols(c)]).astype(BF16)
        gg[0, :, tcols(c)] = jnp.sum(normed * g_ref[:, tcols(c)].astype(F32), axis=0, keepdims=True)
        return 0
    lax.fori_loop(0, width // 128, att_body, 0, unroll=3)

    def gain_copy(number):
        axis, s = gain_stages[number]
        index = me if axis == "seq" else dp
        return pltpu.make_async_remote_copy(
            src_ref=gg.at[2 * number], dst_ref=gg.at[2 * number + 1],
            send_sem=gg_s.at[number], recv_sem=gg_r.at[number],
            device_id={axis: xor_partner(index, s)}, device_id_type=MESH,
        )

    def gain_finish(number):
        gain_copy(number).wait()
        gg[2 * number + 2] = gg[2 * number] + gg[2 * number + 1]

    def backward(g, q_at, d_at, c_at, slot, dq_put, first):
        for j in range(GH):
            h = g * GH + j
            q = q_at[hrows(g, j), :]
            da = d_at[hrows(g, j), :]
            p = e[slot, h] * c_at[g, j:j + 1, :]
            pb = p.astype(BF16)
            dp_ = dot_nn(vh[h], da)
            ds = (p * (dp_ - c_at[g, GH + j:GH + j + 1, :])).astype(BF16)
            dk = dot_nt(q, ds)
            dv = dot_nt(da, pb)
            if first:
                dkt[hrows(g, j), :] = dk
                dvt[hrows(g, j), :] = dv
            else:
                dkt[hrows(g, j), :] += dk
                dvt[hrows(g, j), :] += dv
            dq_put(g, j, dot_nn(kt[hrows(g, j), :], ds) * scale)

    def own_put(g, j, x):
        dqown[hrows(g, j), :] = x

    stages = len(gain_stages)
    gain_copy(0).start()

    def own_bwd(g, _):
        backward(g, qt, dot, cown, OWN, own_put, True)
        return 0
    lax.fori_loop(0, groups, own_bwd, 0)

    def serve_bwd(g, _):
        for i in range(2):
            @to_client(i)
            def _(i=i):
                d_copy(i, g).wait_recv()

            @relays(i)
            def _(i=i):
                df_copy(i, g).start()
        for i in (2, 3, 0, 1):
            @to_client(i)
            def _(i=i):
                c_copy(i, g).wait_recv()
                if i >= 2:
                    d_copy(i, g).wait_recv()

                def put(g, j, x):
                    dqout[i, hrows(g, j), :] = x.astype(BF16)
                backward(g, qin.at[i], doin.at[i], cin.at[i], i, put, False)
            if i >= 2:
                @mated(i)
                def _(i=i):
                    xm_copy(i, g).start()
            else:
                @relays(i)
                def _(i=i):
                    xm_copy(i + 2, g).wait_recv()
                    both = dqout[i, rows(g), :].astype(F32) + dqmate[rows(g), :].astype(F32)
                    dqout[i, rows(g), :] = both.astype(BF16)

            @unmated(i)
            def _(i=i):
                x_copy(i, g).start()
        for number in range(min(groups, stages)):
            @pl.when(g == number)
            def _(number=number):
                gain_finish(number)
                if number + 1 < stages:
                    gain_copy(number + 1).start()
        return 0
    lax.fori_loop(0, groups, serve_bwd, 0)

    for number in range(groups, stages):
        gain_finish(number)
        if number + 1 < stages:
            gain_copy(number + 1).start()
    dg_ref[...] = gg[2 * stages]

    def out_kv(c, _):
        dk_ref[:, tcols(c)] = (dkt[tcols(c), :] * scale).astype(BF16).T
        dv_ref[:, tcols(c)] = dvt[tcols(c), :].astype(BF16).T
        return 0
    lax.fori_loop(0, width // 128, out_kv, 0, unroll=3)

    def out_q(g, _):
        for i in range(NS):
            @direct(i)
            def _(i=i):
                x_copy(i, g).wait_recv()
        for c in range(GW // 128):
            at = tcols(g * (GW // 128) + c)
            acc = dqown[at, :]
            for i in range(NS):
                acc = acc + dqin[i, at, :].astype(F32)
            dq_ref[:, at] = acc.astype(BF16).T
        return 0
    lax.fori_loop(0, groups, out_q, 0)

    def drain(g, _):
        for i in range(NS):
            @to_target(i)
            def _(i=i):
                c_copy(i, g).wait_send()

            @direct(i)
            def _(i=i):
                q_copy(i, g).wait_send()
                d_copy(i, g).wait_send()
            if i < 2:
                @relays(i)
                def _(i=i):
                    qf_copy(i, g).wait_send()
                    df_copy(i, g).wait_send()

            @to_client(i)
            def _(i=i):
                s_copy(i, g).wait_send()

            @unmated(i)
            def _(i=i):
                o_copy(i, g).wait_send()
                x_copy(i, g).wait_send()
            if i >= 2:
                @mated(i)
                def _(i=i):
                    om_copy(i, g).wait_send()
                    sm_copy(i, g).wait_send()
                    xm_copy(i, g).wait_send()
        return 0
    lax.fori_loop(0, groups, drain, 0)
    for i in range(NS):
        @to_target(i)
        def _(i=i):
            b_copy(i).wait_send()


def per_device(sizes, queries, keys, values, grad_out, gain, band_start, band_end):
    toks, width = queries.shape[1:]
    frames = keys.shape[1]
    heads = width // HD
    groups = width // GW
    n_dp, n_seq, n_tensor = sizes
    n_t = len(xor_strides(n_tensor))
    n_g = len(xor_strides(n_seq)) + len(xor_strides(n_dp))
    vm = pltpu.VMEM
    slots = (NS, width, toks)
    rows8 = (groups, 8, toks)
    dma = pltpu.SemaphoreType.DMA
    scratch = [
        vm((width, toks), BF16), vm(slots, BF16), vm((8, 128), jnp.int32), vm((NS, 8, 128), jnp.int32),
        vm((width, frames), BF16), vm((width, frames), BF16),
        vm((heads, frames, HD), BF16), vm((heads, frames, HD), BF16),
        vm((NS + 1, heads, frames, toks), F32),
        vm((width, toks), F32), vm(rows8, F32),
        vm(slots, BF16), vm((NS,) + rows8, F32), vm(slots, BF16), vm((NS,) + rows8, F32),
        vm((width, toks), F32), vm((width, toks), F32), vm((width, toks), BF16),
        vm(rows8, F32), vm((NS,) + rows8, F32), vm(slots, BF16), vm((NS,) + rows8, F32),
        vm((width, toks), F32), vm(slots, BF16), vm(slots, BF16),
        vm((width, frames), F32), vm((width, frames), F32),
        vm((2 * n_t + 1, 16, toks), F32), vm((2 * n_g + 1, 1, width), F32),
        vm((width, toks), F32),
        dma((NS, groups)), dma((NS, groups)), dma((NS,)), dma((NS,)),
    ] + [dma((NS, groups)) for _ in range(10)] + [
        dma((n_t,)), dma((n_t,)), dma((n_g,)), dma((n_g,)), dma((groups,)), dma((groups,)),
        vm((width, toks), BF16), vm(rows8, F32), vm((width, toks), BF16),
    ] + [dma((groups,)) for _ in range(6)
    ]
    vspec = pl.BlockSpec(memory_space=pltpu.VMEM)
    sspec = pl.BlockSpec(memory_space=pltpu.SMEM)
    outs = pl.pallas_call(
        functools.partial(body, sizes),
        out_shape=(
            jax.ShapeDtypeStruct((toks, width), BF16),
            jax.ShapeDtypeStruct((toks, width), BF16),
            jax.ShapeDtypeStruct((frames, width), BF16),
            jax.ShapeDtypeStruct((frames, width), BF16),
            jax.ShapeDtypeStruct((1, width), F32),
        ),
        in_specs=[vspec] * 5 + [sspec] * 2,
        out_specs=(vspec,) * 5,
        scratch_shapes=scratch,
        compiler_params=pltpu.CompilerParams(
            collective_id=0, has_side_effects=True, vmem_limit_bytes=58 * 1024 * 1024
        ),
    )(queries[0], keys[0], values[0], grad_out[0], gain[None], band_start[0], band_end[0])
    attended, grad_q, grad_k, grad_v, grad_gain = outs
    return attended[None], grad_q[None], grad_k[None], grad_v[None], grad_gain[0]


def solution(mesh):
    sizes = (mesh.shape["dp"], mesh.shape["seq"], mesh.shape["tensor"])
    return jax.shard_map(
        functools.partial(per_device, sizes),
        mesh=mesh,
        in_specs=(
            P("dp", "seq", "tensor"),
            P("dp", "seq", "tensor"),
            P("dp", "seq", "tensor"),
            P("dp", "seq", "tensor"),
            P("tensor"),
            P("dp", "seq"),
            P("dp", "seq"),
        ),
        out_specs=(
            P("dp", "seq", "tensor"),
            P("dp", "seq", "tensor"),
            P("dp", "seq", "tensor"),
            P("dp", "seq", "tensor"),
            P("tensor"),
        ),
        check_vma=False,
    )
```
